32 devices in a mesh: parts: 2 (over x), wide: 16 (over z, y, core).
Axes of the slice: x: 2, y: 2, z: 4, core: 2. Of those that a mesh axis runs over, the one named last changes fastest.
Arguments:
- tokens: bfloat16 [8192, 2048], P(('parts', 'wide')), parts along dimension 0, may hold values from -6 to 6
- token_group: int32 [8192], P(('parts', 'wide')), parts along dimension 0, may hold values from 0 to 255, as said below
- group_experts: int32 [512, 1], P(('parts', 'wide')), parts along dimension 0, may hold values from -1 to 15, as said below
- route_ids: int32 [8192, 8], P(('parts', 'wide')), parts along dimension 0, may hold values from 0 to 15, as said below
- route_gates: float32 [8192, 8], P(('parts', 'wide')), parts along dimension 0, may hold values from 0.1 to 1
- w_gate: bfloat16 [16, 2048, 768], P('wide'), may hold values from -0.125 to 0.125
- w_up: bfloat16 [16, 2048, 768], P('wide'), may hold values from -0.125 to 0.125
- w_down: bfloat16 [16, 768, 2048], P('wide'), may hold values from -0.21875 to 0.21875
Outputs:
- mixed: bfloat16 [8192, 2048], P(('parts', 'wide')), parts along dimension 0
The draws below stay inside these ranges and needn't reach their ends.
There are 2 independent parts, one for each index of `parts`. The reference program is written for one: setup_inputs(seed, part) draws one part's arguments, and reference() takes and returns one part's arrays. A program takes and returns all parts, laid end to end along the dimension named above; an argument that names none is the same for every part. Nothing has to cross between parts.
Inputs may be any that keep to these rules, and one draw needn't show every extreme that they name: `token_group`: Nondecreasing. The 256 tokens of index d of wide form groups d * 16 to d * 16 + 15, each a run of 1 to 24 tokens; on every index one group has exactly 24 tokens. `group_experts`: row g holds 2 to 1 distinct experts in its first entries and -1 after them; the groups of one index of wide list disjoint experts; every index has a group of 1 expert holding 24 tokens. Hence at most 24 tokens of one index of wide are kept for one expert, and one expert gets exactly 24 from every index. `route_ids`: each row names 8 distinct experts, among them every expert listed for the token's group.
All inputs are finite; a program needn't handle non-finite values.
Results may differ from the reference program's by a relative error of at most 0.0058.
Values may be sent and summed in bfloat16 or wider, within the bound.
A program may use at most 128 MiB of HBM per device.

```python
import math
import jax
import jax.numpy as jnp
from jax import lax

D = 2048
FF = 768
TOP = 8
GRP_DEV = 16
TOK_DEV = 256
CAP = 24
EXPERTS = 16
LIST = 1
GROUPS = 256
TOKENS = 4096
N_WIDE = 16


def layout(key):
    base = jax.random.fold_in(key, 4242)
    devices = GROUPS // GRP_DEV
    rest = TOK_DEV - CAP
    per = rest // (GRP_DEV - 1)
    extra = rest % (GRP_DEV - 1)
    reach = max(0, min(per - 1, CAP - per - 1))
    pairs = (GRP_DEV - 1) // 2
    others = per + (jnp.arange(GRP_DEV - 1) < extra).astype(jnp.int32)
    shifts = jax.random.randint(jax.random.fold_in(base, 1), (devices, pairs), -reach, reach + 1)
    moved = jnp.stack([shifts, -shifts], axis=2).reshape(devices, 2 * pairs)
    moved = jnp.pad(moved, ((0, 0), (0, GRP_DEV - 1 - 2 * pairs)))
    sizes_first = jnp.concatenate([jnp.full((devices, 1), CAP, jnp.int32), others[None, :] + moved], axis=1)
    group_iota = jnp.arange(GRP_DEV, dtype=jnp.int32)
    order = jnp.argsort(jax.random.randint(jax.random.fold_in(base, 2), (devices, GRP_DEV), 0, 4096) * GRP_DEV + group_iota[None, :], axis=1)
    sizes = jnp.take_along_axis(sizes_first, order, axis=1)
    widest = jnp.argmax((order == 0).astype(jnp.int32), axis=1).astype(jnp.int32)
    ends = jnp.cumsum(sizes, axis=1)
    position = jnp.arange(TOK_DEV, dtype=jnp.int32)
    local = jnp.sum((ends[:, None, :] <= position[None, :, None]).astype(jnp.int32), axis=2)
    token_group = (local + jnp.arange(devices, dtype=jnp.int32)[:, None] * GRP_DEV).reshape(-1).astype(jnp.int32)
    counts = jax.random.randint(jax.random.fold_in(base, 3), (devices, GRP_DEV), max(1, LIST // 2), LIST + 1)
    counts = jnp.where(group_iota[None, :] == widest[:, None], LIST, counts)
    popular = jax.random.permutation(jax.random.fold_in(base, 4), EXPERTS).astype(jnp.int32)
    rank = jnp.argsort(popular).astype(jnp.int32)
    expert_iota = jnp.arange(EXPERTS, dtype=jnp.int32)
    score = jax.random.randint(jax.random.fold_in(base, 5), (devices, EXPERTS), 0, 4096) * (rank[None, :] + 4) // 4
    score = jnp.where(expert_iota[None, :] == popular[0], -1, score * EXPERTS + expert_iota[None, :])
    pick = jnp.argsort(score, axis=1).astype(jnp.int32)
    turn = jnp.where(group_iota[None, :] == widest[:, None], 0, group_iota[None, :] + (group_iota[None, :] < widest[:, None]).astype(jnp.int32))
    offset = jnp.sum(counts[:, None, :] * (turn[:, None, :] < turn[:, :, None]).astype(jnp.int32), axis=2)
    slot = jnp.arange(LIST, dtype=jnp.int32)
    where_at = jnp.minimum(offset[:, :, None] + slot[None, None, :], EXPERTS - 1)
    named = jnp.take_along_axis(pick, where_at.reshape(devices, GRP_DEV * LIST), axis=1).reshape(devices, GRP_DEV, LIST)
    group_experts = jnp.where(slot[None, None, :] < counts[:, :, None], named, -1).reshape(GROUPS, LIST).astype(jnp.int32)
    return (token_group, group_experts)


def draw_token_group(key, part):
    return layout(key)[0]


def draw_group_experts(key, part):
    return layout(key)[1]


def draw_route_ids(key, part):
    token_group, group_experts = layout(key)
    base = jax.random.fold_in(key, 777)
    lists = group_experts[token_group]
    expert_iota = jnp.arange(EXPERTS, dtype=jnp.int32)
    member = jnp.any(lists[:, :, None] == expert_iota[None, None, :], axis=1).astype(jnp.int32)
    score = jax.random.randint(jax.random.fold_in(base, 1), (TOKENS, EXPERTS), 0, 4096) * EXPERTS + expert_iota[None, :] - member * (4096 * EXPERTS)
    chosen = jnp.argsort(score, axis=1)[:, :TOP]
    shuffle = jnp.argsort(jax.random.randint(jax.random.fold_in(base, 2), (TOKENS, TOP), 0, 4096) * TOP + jnp.arange(TOP)[None, :], axis=1)
    return jnp.take_along_axis(chosen, shuffle, axis=1).astype(jnp.int32)


def shard_levels(stream_key, extent, shards, low, high):
    level, own = 1.0, jax.random.fold_in(stream_key, 6)
    for axis_at, blocks in shards:
        draws = jnp.exp(jax.random.uniform(jax.random.fold_in(own, axis_at), (blocks,), jnp.float32, low / len(shards), high / len(shards)))
        level = level * jnp.repeat(draws, extent[axis_at] // blocks).reshape([-1 if axis == axis_at else 1 for axis in range(len(extent))])
    return level


def normal_values(key, extent, deviation, most, pieces=(), kind=jnp.bfloat16):
    values = deviation * jax.random.normal(key, extent, jnp.float32)
    if pieces:
        values = values * shard_levels(key, extent, pieces, -0.22, 0.18)
    return jnp.clip(values, -most, most).astype(kind)


def setup_inputs(seed: int = 0, part: int = 0) -> dict:
    arg_keys = jax.random.split(jax.random.key(seed), 9)
    own_keys = jax.random.split(jax.random.fold_in(arg_keys[8], part), 9)
    tokens = normal_values(own_keys[0], (TOKENS, D), 1.0, 6.0, ((0, 16),))
    token_group = draw_token_group(jax.random.fold_in(jax.random.fold_in(arg_keys[8], part), 71), part)
    group_experts = draw_group_experts(jax.random.fold_in(jax.random.fold_in(arg_keys[8], part), 71), part)
    route_ids = draw_route_ids(jax.random.fold_in(jax.random.fold_in(arg_keys[8], part), 71), part)
    route_gates = jnp.clip(jnp.exp(math.log(1.0) - 2.3025851 * jax.random.uniform(own_keys[4], (TOKENS, TOP), jnp.float32) ** shard_levels(own_keys[4], (TOKENS, TOP), ((0, 16),), -0.2, 0.2)), 0.1, 1.0)
    w_gate = normal_values(arg_keys[5], (EXPERTS, D, FF), D ** -0.5, 0.125, ((0, 16),))
    w_up = normal_values(arg_keys[6], (EXPERTS, D, FF), D ** -0.5, 0.125, ((0, 16),))
    w_down = normal_values(arg_keys[7], (EXPERTS, FF, D), FF ** -0.5, 0.21875, ((0, 16),))
    return {"tokens": tokens, "token_group": token_group, "group_experts": group_experts, "route_ids": route_ids, "route_gates": route_gates, "w_gate": w_gate, "w_up": w_up, "w_down": w_down}


def expert_rows(rows, gate_w, up_w, down_w):
    gate = jnp.dot(rows, gate_w, preferred_element_type=jnp.float32)
    upper = jnp.dot(rows, up_w, preferred_element_type=jnp.float32)
    hidden = (jax.nn.silu(gate) * upper).astype(jnp.bfloat16)
    return jnp.dot(hidden, down_w, preferred_element_type=jnp.float32).astype(jnp.bfloat16)


def reference(tokens, token_group, group_experts, route_ids, route_gates, w_gate, w_up, w_down):
    group_iota = jnp.arange(GROUPS, dtype=jnp.int32)
    sizes = jnp.sum((token_group[:, None] == group_iota[None, :]).astype(jnp.int32), axis=0)
    starts = jnp.cumsum(sizes) - sizes
    sizes_dev = sizes.reshape(N_WIDE, GRP_DEV)
    starts_dev = starts.reshape(N_WIDE, GRP_DEV)
    lists = group_experts.reshape(N_WIDE, GRP_DEV, LIST)
    slot_iota = jnp.arange(CAP, dtype=jnp.int32)

    def one_expert(total, expert):
        listed = jnp.any(lists == expert, axis=2).astype(jnp.int32)
        run_start = jnp.sum(listed * starts_dev, axis=1)
        run_size = jnp.sum(listed * sizes_dev, axis=1)
        rows = run_start[:, None] + slot_iota[None, :]
        live = (slot_iota[None, :] < run_size[:, None]).reshape(-1)
        rows = jnp.minimum(rows, TOKENS - 1).reshape(-1).astype(jnp.int32)
        picked = tokens[rows]
        result = expert_rows(picked, w_gate[expert], w_up[expert], w_down[expert])
        weight = jnp.sum(jnp.where(route_ids[rows] == expert, route_gates[rows], jnp.zeros((), route_gates.dtype)), axis=1)
        weight = jnp.where(live, weight, jnp.zeros((), weight.dtype))
        return total.at[rows].add(weight[:, None] * result.astype(weight.dtype)), None

    start_total = jnp.zeros((TOKENS, D), route_gates.dtype)
    total, unused = lax.scan(one_expert, start_total, jnp.arange(EXPERTS, dtype=jnp.int32))
    return total.astype(jnp.bfloat16)
```

```python
import functools

import jax
import jax.numpy as jnp
from jax import lax
from jax.experimental import pallas as pl
from jax.experimental.pallas import tpu as pltpu
from jax.sharding import PartitionSpec as P

CAP = 24
MESH = pl.DeviceIdType.MESH
SEND_ORDER = (3, 2, 1, 0)
WORK_ORDER = (3, 2, 1, 0)
TAKE_ORDER = (3, 2, 1, 0)


def partner(me, distance):
    other = me
    bit = 1
    while bit <= distance:
        if distance & bit:
            other = other + bit * (1 - 2 * (lax.div(me, bit) % 2))
        bit *= 2
    return other


def kernel(
    n, chunks, tokens_ref, group_ref, listed_ref, ids_ref, gates_ref, gate_hbm, up_hbm, down_hbm, out_ref,
    gate_w, up_w, down_w, outgoing, arrived, results, back, hidden, total, weight_sem, send_a, recv_a, send_b, recv_b,
):
    me = lax.axis_index("wide")
    count, width = tokens_ref.shape
    groups, lists = listed_ref.shape
    per = n // chunks
    rows = per * CAP
    inner = hidden.shape[1]

    barrier = pltpu.get_barrier_semaphore()
    for d in range(1, n):
        pl.semaphore_signal(barrier, inc=1, device_id={"wide": partner(me, d)}, device_id_type=MESH)
    loads = [
        pltpu.make_async_copy(src.at[0], dst, weight_sem.at[i])
        for i, (src, dst) in enumerate(((gate_hbm, gate_w), (up_hbm, up_w), (down_hbm, down_w)))
    ]

    local = group_ref[...] - me * groups
    group_iota = lax.broadcasted_iota(jnp.int32, (groups, count), 0)
    in_group = local == group_iota
    starts = jnp.sum((local < group_iota).astype(jnp.float32), axis=1, keepdims=True)
    start_row = jnp.sum(jnp.where(in_group, starts, 0.0), axis=0, keepdims=True).astype(jnp.int32)
    slot_row = lax.broadcasted_iota(jnp.int32, (1, count), 1) - start_row
    experts, targets = [], []
    for index in range(lists):
        named = listed_ref[:, index : index + 1].astype(jnp.float32) + 1.0
        expert = jnp.sum(jnp.where(in_group, named, 0.0), axis=0, keepdims=True).astype(jnp.int32) - 1
        block = jnp.bitwise_xor(expert, jnp.full((1, count), me, jnp.int32))
        experts.append(expert)
        targets.append(jnp.where(expert >= 0, block * CAP + slot_row, -1))

    def copy(phase, d):
        src, dst, send, recv = ((outgoing, arrived, send_a, recv_a), (results, back, send_b, recv_b))[phase]
        return pltpu.make_async_remote_copy(
            src_ref=src.at[d],
            dst_ref=dst.at[d],
            send_sem=send.at[d],
            recv_sem=recv.at[d],
            device_id={"wide": partner(me, d)},
            device_id_type=MESH,
        )

    def members(c):
        return [d for d in range(c * per, (c + 1) * per) if d > 0]

    greeted = False
    for c in SEND_ORDER:
        row_iota = lax.broadcasted_iota(jnp.int32, (rows, count), 0) + c * rows
        pick = sum((row_iota == target).astype(jnp.float32) for target in targets).astype(jnp.bfloat16)
        tile = min(width, 512)

        def pack(j, carry):
            cols = pl.ds(pl.multiple_of(j * tile, tile), tile)
            picked = jnp.dot(pick, tokens_ref[:, cols], preferred_element_type=jnp.float32)
            outgoing[pl.ds(c * per, per), :, cols] = picked.reshape(per, CAP, tile).astype(jnp.bfloat16)
            return carry

        lax.fori_loop(0, width // tile, pack, 0)
        if not greeted:
            pl.semaphore_wait(barrier, n - 1)
            greeted = True
        for d in reversed(members(c)):
            copy(0, d).start()
    for load in loads:
        load.start()
    own = pltpu.make_async_copy(outgoing.at[0], arrived.at[0], weight_sem.at[3])
    own.start()

    columns = []
    for index in range(lists):
        target = jnp.transpose(jnp.broadcast_to(targets[index].astype(jnp.float32), (128, count)))[:, :1]
        expert = jnp.transpose(jnp.broadcast_to(experts[index].astype(jnp.float32), (128, count)))[:, :1]
        expert = expert.astype(jnp.int32)
        chosen = jnp.where(ids_ref[...] == expert, gates_ref[...], 0.0)
        weight = jnp.where(expert >= 0, jnp.sum(chosen, axis=1, keepdims=True), 0.0)
        columns.append((target.astype(jnp.int32), weight))

    loaded = False
    for c in WORK_ORDER:
        for d in members(c):
            copy(0, d).wait_recv()
        if c == 0:
            own.wait()
        if not loaded:
            for load in loads:
                load.wait()
            loaded = True

        def raise_(j, carry):
            cols = pl.ds(pl.multiple_of(j * 256, 256), 256)
            x = arrived[pl.ds(c * per, per)].reshape(rows, width)
            gate = jnp.dot(x, gate_w[:, cols], preferred_element_type=jnp.float32)
            upper = jnp.dot(x, up_w[:, cols], preferred_element_type=jnp.float32)
            hidden[:, cols] = (gate / (1.0 + jnp.exp(-gate)) * upper).astype(jnp.bfloat16)
            return carry

        lax.fori_loop(0, inner // 256, raise_, 0)

        def lower(j, carry):
            cols = pl.ds(pl.multiple_of(j * 512, 512), 512)
            y = jnp.dot(hidden[...], down_w[:, cols], preferred_element_type=jnp.float32)
            results[pl.ds(c * per, per), :, cols] = y.reshape(per, CAP, 512).astype(jnp.bfloat16)
            return carry

        lax.fori_loop(0, width // 512, lower, 0)
        for d in reversed(members(c)):
            copy(1, d).start()

    for place, c in enumerate(TAKE_ORDER):
        for d in members(c):
            copy(1, d).wait_recv()
        lane_iota = lax.broadcasted_iota(jnp.int32, (count, rows), 1) + c * rows
        picks = [((lane_iota == target).astype(jnp.bfloat16), weight) for target, weight in columns]

        def take(j, carry):
            cols = pl.ds(pl.multiple_of(j * 512, 512), 512)
            own_results = results if c == 0 else None
            y = back[pl.ds(c * per, per), :, cols]
            if own_results is not None:
                y = jnp.concatenate([results[pl.ds(0, 1), :, cols], back[pl.ds(1, per - 1), :, cols]], axis=0)
            y = y.reshape(rows, 512)
            mix = sum(weight * jnp.dot(pick, y, preferred_element_type=jnp.float32) for pick, weight in picks)
            if place > 0:
                mix = mix + total[:, cols]
            if place < chunks - 1:
                total[:, cols] = mix
            else:
                out_ref[:, cols] = mix.astype(jnp.bfloat16)
            return carry

        lax.fori_loop(0, width // 512, take, 0)
    for d in range(1, n):
        copy(0, d).wait_send()
        copy(1, d).wait_send()


def on_device(tokens, token_group, group_experts, route_ids, route_gates, w_gate, w_up, w_down):
    n = lax.axis_size("wide")
    count, width = tokens.shape
    inner = w_gate.shape[2]
    chunks = 4
    vmem = pl.BlockSpec(memory_space=pltpu.VMEM)
    hbm = pl.BlockSpec(memory_space=pl.ANY)
    blocks = pltpu.VMEM((n, CAP, width), jnp.bfloat16)
    return pl.pallas_call(
        functools.partial(kernel, n, chunks),
        out_shape=jax.ShapeDtypeStruct((count, width), jnp.bfloat16),
        in_specs=[vmem] * 5 + [hbm] * 3,
        out_specs=vmem,
        scratch_shapes=[
            pltpu.VMEM((width, inner), jnp.bfloat16),
            pltpu.VMEM((width, inner), jnp.bfloat16),
            pltpu.VMEM((inner, width), jnp.bfloat16),
            blocks,
            blocks,
            blocks,
            blocks,
            pltpu.VMEM((n // chunks * CAP, inner), jnp.bfloat16),
            pltpu.VMEM((count, width), jnp.float32),
            pltpu.SemaphoreType.DMA((4,)),
            pltpu.SemaphoreType.DMA((n,)),
            pltpu.SemaphoreType.DMA((n,)),
            pltpu.SemaphoreType.DMA((n,)),
            pltpu.SemaphoreType.DMA((n,)),
        ],
        compiler_params=pltpu.CompilerParams(
            collective_id=0, has_side_effects=True, vmem_limit_bytes=56 * 1024 * 1024
        ),
        cost_estimate=pl.CostEstimate(
            flops=6 * n * CAP * width * inner, bytes_accessed=6 * width * inner + 4 * count * width,
            transcendentals=n * CAP * inner,
        ),
    )(tokens, token_group.reshape(1, count), group_experts, route_ids, route_gates, w_gate, w_up, w_down)


def solution(mesh):
    in_specs = (
        P(("parts", "wide"), None),
        P(("parts", "wide")),
        P(("parts", "wide"), None),
        P(("parts", "wide"), None),
        P(("parts", "wide"), None),
        P("wide", None, None),
        P("wide", None, None),
        P("wide", None, None),
    )
    out_specs = P(("parts", "wide"), None)
    return jax.shard_map(
        on_device, mesh=mesh, in_specs=in_specs, out_specs=out_specs, check_vma=False
    )
```

```python
import functools

import jax
import jax.numpy as jnp
from jax import lax
from jax.experimental import pallas as pl
from jax.experimental.pallas import tpu as pltpu
from jax.sharding import PartitionSpec as P

CAP = 24
MESH = pl.DeviceIdType.MESH
SEND_ORDER = (2, 3, 1, 0)
WORK_ORDER = (2, 1, 3, 0)
TAKE_ORDER = (1, 2, 0, 3)


def partner(me, distance):
    other = me
    bit = 1
    while bit <= distance:
        if distance & bit:
            other = other + bit * (1 - 2 * (lax.div(me, bit) % 2))
        bit *= 2
    return other


def kernel(
    n, chunks, tokens_ref, group_ref, listed_ref, ids_ref, gates_ref, gate_hbm, up_hbm, down_hbm, out_ref,
    gate_w, up_w, down_w, outgoing, arrived, results, back, hidden, total, weight_sem, send_a, recv_a, send_b, recv_b,
):
    me = lax.axis_index("wide")
    count, width = tokens_ref.shape
    lists, groups = listed_ref.shape
    per = n // chunks
    rows = per * CAP
    inner = hidden.shape[1]

    barrier = pltpu.get_barrier_semaphore()
    for d in range(1, n):
        pl.semaphore_signal(barrier, inc=1, device_id={"wide": partner(me, d)}, device_id_type=MESH)
    loads = [
        pltpu.make_async_copy(src.at[0], dst, weight_sem.at[i])
        for i, (src, dst) in enumerate(((gate_hbm, gate_w), (up_hbm, up_w), (down_hbm, down_w)))
    ]

    local = group_ref[...] - me * groups
    group_iota = lax.broadcasted_iota(jnp.int32, (groups, count), 0)
    in_group = local == group_iota
    starts = jnp.sum((local < group_iota).astype(jnp.float32), axis=1, keepdims=True)
    start_row = jnp.sum(jnp.where(in_group, starts, 0.0), axis=0, keepdims=True).astype(jnp.int32)
    slot_row = lax.broadcasted_iota(jnp.int32, (1, count), 1) - start_row
    diagonal = lax.broadcasted_iota(jnp.int32, (groups, groups), 0) == lax.broadcasted_iota(
        jnp.int32, (groups, groups), 1
    )
    experts, targets = [], []
    for index in range(lists):
        named = jnp.sum(
            jnp.where(diagonal, listed_ref[index : index + 1, :].astype(jnp.float32) + 1.0, 0.0), axis=1, keepdims=True
        )
        expert = jnp.sum(jnp.where(in_group, named, 0.0), axis=0, keepdims=True).astype(jnp.int32) - 1
        block = jnp.bitwise_xor(expert, jnp.full((1, count), me, jnp.int32))
        experts.append(expert)
        targets.append(jnp.where(expert >= 0, block * CAP + slot_row, -1))

    def copy(phase, d):
        src, dst, send, recv = ((outgoing, arrived, send_a, recv_a), (results, back, send_b, recv_b))[phase]
        return pltpu.make_async_remote_copy(
            src_ref=src.at[d],
            dst_ref=dst.at[d],
            send_sem=send.at[d],
            recv_sem=recv.at[d],
            device_id={"wide": partner(me, d)},
            device_id_type=MESH,
        )

    def members(c):
        return [d for d in range(c * per, (c + 1) * per) if d > 0]

    greeted = False
    for c in SEND_ORDER:
        row_iota = lax.broadcasted_iota(jnp.int32, (rows, count), 0) + c * rows
        pick = sum((row_iota == target).astype(jnp.float32) for target in targets).astype(jnp.bfloat16)
        tile = min(width, 512)

        def pack(j, carry):
            cols = pl.ds(pl.multiple_of(j * tile, tile), tile)
            picked = jnp.dot(pick, tokens_ref[:, cols], preferred_element_type=jnp.float32)
            outgoing[pl.ds(c * per, per), :, cols] = picked.reshape(per, CAP, tile).astype(jnp.bfloat16)
            return carry

        lax.fori_loop(0, width // tile, pack, 0)
        if not greeted:
            pl.semaphore_wait(barrier, n - 1)
            greeted = True
        for d in reversed(members(c)):
            copy(0, d).start()
    for load in loads:
        load.start()
    own = pltpu.make_async_copy(outgoing.at[0], arrived.at[0], weight_sem.at[3])
    own.start()

    columns = []
    for index in range(lists):
        chosen = jnp.where(ids_ref[...] == experts[index], gates_ref[...], 0.0)
        weight = jnp.where(experts[index] >= 0, jnp.sum(chosen, axis=0, keepdims=True), 0.0)
        weight = jnp.transpose(jnp.broadcast_to(weight, (128, count)))[:, :1]
        target = jnp.transpose(jnp.broadcast_to(targets[index].astype(jnp.float32), (128, count)))[:, :1]
        columns.append((target.astype(jnp.int32), weight))

    loaded = False
    for c in WORK_ORDER:
        for d in members(c):
            copy(0, d).wait_recv()
        if c == 0:
            own.wait()
        if not loaded:
            for load in loads:
                load.wait()
            loaded = True

        def raise_(j, carry):
            cols = pl.ds(pl.multiple_of(j * 256, 256), 256)
            x = arrived[pl.ds(c * per, per)].reshape(rows, width)
            gate = jnp.dot(x, gate_w[:, cols], preferred_element_type=jnp.float32)
            upper = jnp.dot(x, up_w[:, cols], preferred_element_type=jnp.float32)
            hidden[:, cols] = (gate / (1.0 + jnp.exp(-gate)) * upper).astype(jnp.bfloat16)
            return carry

        lax.fori_loop(0, inner // 256, raise_, 0)

        def lower(j, carry):
            cols = pl.ds(pl.multiple_of(j * 512, 512), 512)
            y = jnp.dot(hidden[...], down_w[:, cols], preferred_element_type=jnp.float32)
            results[pl.ds(c * per, per), :, cols] = y.reshape(per, CAP, 512).astype(jnp.bfloat16)
            return carry

        lax.fori_loop(0, width // 512, lower, 0)
        for d in reversed(members(c)):
            copy(1, d).start()

    for place, c in enumerate(TAKE_ORDER):
        for d in members(c):
            copy(1, d).wait_recv()
        lane_iota = lax.broadcasted_iota(jnp.int32, (count, rows), 1) + c * rows
        picks = [((lane_iota == target).astype(jnp.bfloat16), weight) for target, weight in columns]

        def take(j, carry):
            cols = pl.ds(pl.multiple_of(j * 512, 512), 512)
            own_results = results if c == 0 else None
            y = back[pl.ds(c * per, per), :, cols]
            if own_results is not None:
                y = jnp.concatenate([results[pl.ds(0, 1), :, cols], back[pl.ds(1, per - 1), :, cols]], axis=0)
            y = y.reshape(rows, 512)
            mix = sum(weight * jnp.dot(pick, y, preferred_element_type=jnp.float32) for pick, weight in picks)
            if place > 0:
                mix = mix + total[:, cols]
            if place < chunks - 1:
                total[:, cols] = mix
            else:
                out_ref[:, cols] = mix.astype(jnp.bfloat16)
            return carry

        lax.fori_loop(0, width // 512, take, 0)
    for d in range(1, n):
        copy(0, d).wait_send()
        copy(1, d).wait_send()


def on_device(tokens, token_group, group_experts, route_ids, route_gates, w_gate, w_up, w_down):
    n = lax.axis_size("wide")
    count, width = tokens.shape
    inner = w_gate.shape[2]
    chunks = 4
    vmem = pl.BlockSpec(memory_space=pltpu.VMEM)
    hbm = pl.BlockSpec(memory_space=pl.ANY)
    blocks = pltpu.VMEM((n, CAP, width), jnp.bfloat16)
    return pl.pallas_call(
        functools.partial(kernel, n, chunks),
        out_shape=pltpu.VMEM((count, width), jnp.bfloat16),
        in_specs=[vmem] * 5 + [hbm] * 3,
        out_specs=vmem,
        scratch_shapes=[
            pltpu.VMEM((width, inner), jnp.bfloat16),
            pltpu.VMEM((width, inner), jnp.bfloat16),
            pltpu.VMEM((inner, width), jnp.bfloat16),
            blocks,
            blocks,
            blocks,
            blocks,
            pltpu.VMEM((n // chunks * CAP, inner), jnp.bfloat16),
            pltpu.VMEM((count, width), jnp.float32),
            pltpu.SemaphoreType.DMA((4,)),
            pltpu.SemaphoreType.DMA((n,)),
            pltpu.SemaphoreType.DMA((n,)),
            pltpu.SemaphoreType.DMA((n,)),
            pltpu.SemaphoreType.DMA((n,)),
        ],
        compiler_params=pltpu.CompilerParams(
            collective_id=0, has_side_effects=True, vmem_limit_bytes=56 * 1024 * 1024
        ),
        cost_estimate=pl.CostEstimate(
            flops=6 * n * CAP * width * inner, bytes_accessed=6 * width * inner + 4 * count * width,
            transcendentals=n * CAP * inner,
        ),
    )(tokens, token_group.reshape(1, count), group_experts.T, route_ids.T, route_gates.T, w_gate, w_up, w_down)


def solution(mesh):
    in_specs = (
        P(("parts", "wide"), None),
        P(("parts", "wide")),
        P(("parts", "wide"), None),
        P(("parts", "wide"), None),
        P(("parts", "wide"), None),
        P("wide", None, None),
        P("wide", None, None),
        P("wide", None, None),
    )
    out_specs = P(("parts", "wide"), None)
    return jax.shard_map(
        on_device, mesh=mesh, in_specs=in_specs, out_specs=out_specs, check_vma=False
    )
```

```python
import functools

import jax
import jax.numpy as jnp
from jax import lax
from jax.experimental import pallas as pl
from jax.experimental.pallas import tpu as pltpu
from jax.sharding import PartitionSpec as P

CAP = 24
MESH = pl.DeviceIdType.MESH
SEND_ORDER = (2, 3, 1, 0)
WORK_ORDER = (2, 1, 0, 3)
TAKE_ORDER = (1, 0, 2, 3)


def partner(me, distance):
    other = me
    bit = 1
    while bit <= distance:
        if distance & bit:
            other = other + bit * (1 - 2 * (lax.div(me, bit) % 2))
        bit *= 2
    return other


def kernel(
    n, chunks, tokens_ref, group_ref, listed_ref, ids_ref, gates_ref, gate_hbm, up_hbm, down_hbm, out_ref,
    gate_w, up_w, down_w, outgoing, arrived, results, back, hidden, total, weight_sem, send_a, recv_a, send_b, recv_b,
):
    me = lax.axis_index("wide")
    count, width = tokens_ref.shape
    lists, groups = listed_ref.shape
    per = n // chunks
    rows = per * CAP
    inner = hidden.shape[1]

    barrier = pltpu.get_barrier_semaphore()
    for d in range(1, n):
        pl.semaphore_signal(barrier, inc=1, device_id={"wide": partner(me, d)}, device_id_type=MESH)
    loads = [
        pltpu.make_async_copy(src.at[0], dst, weight_sem.at[i])
        for i, (src, dst) in enumerate(((gate_hbm, gate_w), (up_hbm, up_w), (down_hbm, down_w)))
    ]

    local = group_ref[...] - me * groups
    group_iota = lax.broadcasted_iota(jnp.int32, (groups, count), 0)
    in_group = local == group_iota
    starts = jnp.sum((local < group_iota).astype(jnp.float32), axis=1, keepdims=True)
    start_row = jnp.sum(jnp.where(in_group, starts, 0.0), axis=0, keepdims=True).astype(jnp.int32)
    slot_row = lax.broadcasted_iota(jnp.int32, (1, count), 1) - start_row
    diagonal = lax.broadcasted_iota(jnp.int32, (groups, groups), 0) == lax.broadcasted_iota(
        jnp.int32, (groups, groups), 1
    )
    experts, targets = [], []
    for index in range(lists):
        named = jnp.sum(
            jnp.where(diagonal, listed_ref[index : index + 1, :].astype(jnp.float32) + 1.0, 0.0), axis=1, keepdims=True
        )
        expert = jnp.sum(jnp.where(in_group, named, 0.0), axis=0, keepdims=True).astype(jnp.int32) - 1
        block = jnp.bitwise_xor(expert, jnp.full((1, count), me, jnp.int32))
        experts.append(expert)
        targets.append(jnp.where(expert >= 0, block * CAP + slot_row, -1))

    def copy(phase, d):
        src, dst, send, recv = ((outgoing, arrived, send_a, recv_a), (results, back, send_b, recv_b))[phase]
        return pltpu.make_async_remote_copy(
            src_ref=src.at[d],
            dst_ref=dst.at[d],
            send_sem=send.at[d],
            recv_sem=recv.at[d],
            device_id={"wide": partner(me, d)},
            device_id_type=MESH,
        )

    def members(c):
        return [d for d in range(c * per, (c + 1) * per) if d > 0]

    greeted = False
    for c in SEND_ORDER:
        row_iota = lax.broadcasted_iota(jnp.int32, (rows, count), 0) + c * rows
        pick = sum((row_iota == target).astype(jnp.float32) for target in targets).astype(jnp.bfloat16)
        tile = min(width, 512)

        def pack(j, carry):
            cols = pl.ds(pl.multiple_of(j * tile, tile), tile)
            picked = jnp.dot(pick, tokens_ref[:, cols], preferred_element_type=jnp.float32)
            outgoing[pl.ds(c * per, per), :, cols] = picked.reshape(per, CAP, tile).astype(jnp.bfloat16)
            return carry

        lax.fori_loop(0, width // tile, pack, 0)
        if not greeted:
            pl.semaphore_wait(barrier, n - 1)
            greeted = True
        for d in reversed(members(c)):
            copy(0, d).start()
    for load in loads:
        load.start()
    own = pltpu.make_async_copy(outgoing.at[0], arrived.at[0], weight_sem.at[3])
    own.start()

    columns = []
    for index in range(lists):
        chosen = jnp.where(ids_ref[...] == experts[index], gates_ref[...], 0.0)
        weight = jnp.where(experts[index] >= 0, jnp.sum(chosen, axis=0, keepdims=True), 0.0)
        weight = jnp.transpose(jnp.broadcast_to(weight, (128, count)))[:, :1]
        target = jnp.transpose(jnp.broadcast_to(targets[index].astype(jnp.float32), (128, count)))[:, :1]
        columns.append((target.astype(jnp.int32), weight))

    loaded = False
    for c in WORK_ORDER:
        for d in members(c):
            copy(0, d).wait_recv()
        if c == 0:
            own.wait()
        if not loaded:
            for load in loads:
                load.wait()
            loaded = True

        def raise_(j, carry):
            cols = pl.ds(pl.multiple_of(j * 256, 256), 256)
            x = arrived[pl.ds(c * per, per)].reshape(rows, width)
            gate = jnp.dot(x, gate_w[:, cols], preferred_element_type=jnp.float32)
            upper = jnp.dot(x, up_w[:, cols], preferred_element_type=jnp.float32)
            hidden[:, cols] = (gate / (1.0 + jnp.exp(-gate)) * upper).astype(jnp.bfloat16)
            return carry

        lax.fori_loop(0, inner // 256, raise_, 0)

        def lower(j, carry):
            cols = pl.ds(pl.multiple_of(j * 512, 512), 512)
            y = jnp.dot(hidden[...], down_w[:, cols], preferred_element_type=jnp.float32)
            results[pl.ds(c * per, per), :, cols] = y.reshape(per, CAP, 512).astype(jnp.bfloat16)
            return carry

        lax.fori_loop(0, width // 512, lower, 0)
        for d in reversed(members(c)):
            copy(1, d).start()

    for place, c in enumerate(TAKE_ORDER):
        for d in members(c):
            copy(1, d).wait_recv()
        lane_iota = lax.broadcasted_iota(jnp.int32, (count, rows), 1) + c * rows
        picks = [((lane_iota == target).astype(jnp.bfloat16), weight) for target, weight in columns]

        def take(j, carry):
            cols = pl.ds(pl.multiple_of(j * 512, 512), 512)
            own_results = results if c == 0 else None
            y = back[pl.ds(c * per, per), :, cols]
            if own_results is not None:
                y = jnp.concatenate([results[pl.ds(0, 1), :, cols], back[pl.ds(1, per - 1), :, cols]], axis=0)
            y = y.reshape(rows, 512)
            mix = sum(weight * jnp.dot(pick, y, preferred_element_type=jnp.float32) for pick, weight in picks)
            if place > 0:
                mix = mix + total[:, cols]
            if place < chunks - 1:
                total[:, cols] = mix
            else:
                out_ref[:, cols] = mix.astype(jnp.bfloat16)
            return carry

        lax.fori_loop(0, width // 512, take, 0)
    for d in range(1, n):
        copy(0, d).wait_send()
        copy(1, d).wait_send()


def on_device(tokens, token_group, group_experts, route_ids, route_gates, w_gate, w_up, w_down):
    n = lax.axis_size("wide")
    count, width = tokens.shape
    inner = w_gate.shape[2]
    chunks = 4
    vmem = pl.BlockSpec(memory_space=pltpu.VMEM)
    hbm = pl.BlockSpec(memory_space=pl.ANY)
    blocks = pltpu.VMEM((n, CAP, width), jnp.bfloat16)
    return pl.pallas_call(
        functools.partial(kernel, n, chunks),
        out_shape=pltpu.VMEM((count, width), jnp.bfloat16),
        in_specs=[vmem] * 5 + [hbm] * 3,
        out_specs=vmem,
        scratch_shapes=[
            pltpu.VMEM((width, inner), jnp.bfloat16),
            pltpu.VMEM((width, inner), jnp.bfloat16),
            pltpu.VMEM((inner, width), jnp.bfloat16),
            blocks,
            blocks,
            blocks,
            blocks,
            pltpu.VMEM((n // chunks * CAP, inner), jnp.bfloat16),
            pltpu.VMEM((count, width), jnp.float32),
            pltpu.SemaphoreType.DMA((4,)),
            pltpu.SemaphoreType.DMA((n,)),
            pltpu.SemaphoreType.DMA((n,)),
            pltpu.SemaphoreType.DMA((n,)),
            pltpu.SemaphoreType.DMA((n,)),
        ],
        compiler_params=pltpu.CompilerParams(
            collective_id=0, has_side_effects=True, vmem_limit_bytes=56 * 1024 * 1024
        ),
        cost_estimate=pl.CostEstimate(
            flops=6 * n * CAP * width * inner, bytes_accessed=6 * width * inner + 4 * count * width,
            transcendentals=n * CAP * inner,
        ),
    )(tokens, token_group.reshape(1, count), group_experts.T, route_ids.T, route_gates.T, w_gate, w_up, w_down)


def solution(mesh):
    in_specs = (
        P(("parts", "wide"), None),
        P(("parts", "wide")),
        P(("parts", "wide"), None),
        P(("parts", "wide"), None),
        P(("parts", "wide"), None),
        P("wide", None, None),
        P("wide", None, None),
        P("wide", None, None),
    )
    out_specs = P(("parts", "wide"), None)
    return jax.shard_map(
        on_device, mesh=mesh, in_specs=in_specs, out_specs=out_specs, check_vma=False
    )
```
